128 devices in a mesh: grp: 4 (over y_lo, core), dev: 32 (over y_hi, z, x).
Axes of the slice: x: 4, y: 4 (y_hi: 2, y_lo: 2; y = y_hi * 2 + y_lo), z: 4, core: 2. Of those that a mesh axis runs over, the one named last changes fastest.
Arguments:
- queries: bfloat16 [65536, 4096], P(('grp', 'dev')), may hold values from -0.3125 to 0.3125
- documents: bfloat16 [65536, 4096], P(('grp', 'dev')), may hold values from -0.3125 to 0.3125
- pair_index: int32 [128, 512], P(('grp', 'dev')), may hold values from 0 to 511, each once within a row
Outputs:
- query_grad: bfloat16 [65536, 4096], P(('grp', 'dev'))
- doc_grad: bfloat16 [65536, 4096], P(('grp', 'dev'))
- row_loss: float32 [65536], P(('grp', 'dev'))
- column_loss: float32 [65536], P(('grp', 'dev'))
The draws below stay inside these ranges and needn't reach their ends.
Inputs may be any that keep to these rules, and one draw needn't show every extreme that they name: Each row of pair_index is a permutation of 0 to 511: query r of block b pairs with document b * 512 + pair_index[b, r].
All inputs are finite; a program needn't handle non-finite values.
Results may differ from the reference program's by a relative error of at most 0.0034.
Values may be sent and summed in bfloat16 or wider, within the bound.
A program may use at most 128 MiB of HBM per device.

```python
import math
import jax
import jax.numpy as jnp
from jax import lax

D = 4096
ROWS = 512
BLOCKS = 128
TOTAL = 65536
GRP_STRIDE = 32
DEV_STRIDE = 16


def shared_parts(key):
    sign_key, power_key = jax.random.split(key)
    sign_vector = jnp.where(jax.random.normal(sign_key, (D,), jnp.float32) > 0.0, 1.0, -1.0)
    strength = jax.random.uniform(power_key, (BLOCKS,), jnp.float32, 0.85, 1.0)
    strength = strength / jnp.max(strength)
    return (sign_vector, strength)


def finish(scale_key, noise_draw, sign_vector, strength, aligned_share):
    row_total = BLOCKS * ROWS
    scales = jnp.exp(jax.random.uniform(scale_key, (row_total, 1), jnp.float32, math.log(0.9), math.log(1.1)))
    values = jnp.clip(0.03 * noise_draw * scales, -0.3125, 0.3125)
    row_ids = jnp.arange(row_total)
    within = row_ids % ROWS
    block_ids = row_ids // ROWS
    strength_row = strength[block_ids] * jnp.where(within >= 2, 0.9, 1.0)
    columns = jnp.arange(D)
    damping = jnp.where((within[:, None] % 2 == 1) & (columns[None, :] < 3), 0.6, 1.0)
    aligned = 0.3125 * sign_vector[None, :] * strength_row[:, None] * damping
    chosen = (within < 4) & (aligned_share > 0.5)
    return jnp.where(chosen[:, None], aligned, values)


def draw_queries(key, part):
    sign_vector, strength = shared_parts(key)
    key = jax.random.fold_in(key, 5)
    scale_key, noise_key = jax.random.split(key)
    noise_draw = jnp.clip(jax.random.normal(noise_key, (BLOCKS * ROWS, D), jnp.float32), -4.0, 4.0)
    return finish(scale_key, noise_draw, sign_vector, strength, 0.0).astype(jnp.bfloat16)


def draw_documents(key, part):
    sign_vector, strength = shared_parts(key)
    key = jax.random.fold_in(key, 6)
    scale_key, noise_key = jax.random.split(key)
    noise_draw = jnp.clip(jax.random.normal(noise_key, (BLOCKS * ROWS, D), jnp.float32), -4.0, 4.0)
    return finish(scale_key, noise_draw, sign_vector, strength, 0.0).astype(jnp.bfloat16)


def setup_inputs(seed: int = 0) -> dict:
    arg_keys = jax.random.split(jax.random.key(seed), 4)
    return {
        "queries": draw_queries(jax.random.fold_in(arg_keys[3], 71), 0),
        "documents": draw_documents(jax.random.fold_in(arg_keys[3], 71), 0),
        "pair_index": jax.vmap(lambda own: jax.random.permutation(own, ROWS))(jax.random.split(arg_keys[2], BLOCKS)).reshape((BLOCKS, ROWS)).astype(jnp.int32),
    }


logit_scale = 20.0


def tile_of(left_rows, right_rows):
    return logit_scale * jnp.dot(left_rows, right_rows.T, preferred_element_type=jnp.float32)


def log_sum(values, along):
    maximum = jnp.max(values, axis=along, keepdims=True)
    return jnp.squeeze(maximum, axis=along) + jnp.log(jnp.sum(jnp.exp(values - maximum), axis=along))


def grad_tile(tile_now, row_stat, column_stat):
    return jnp.exp(tile_now - row_stat[:, None]) + jnp.exp(tile_now - column_stat[None, :])


def rounded_share(values):
    return lax.optimization_barrier(values.astype(jnp.bfloat16)).astype(jnp.float32)


def reference(queries, documents, pair_index):
    query_blocks = queries.reshape(BLOCKS, ROWS, D)
    doc_blocks = documents.reshape(BLOCKS, ROWS, D)
    block_ids = jnp.arange(BLOCKS, dtype=jnp.int32)

    def statistics(block_index):
        first_partner = jnp.bitwise_xor(block_index, GRP_STRIDE)
        second_partner = jnp.bitwise_xor(block_index, DEV_STRIDE)
        own_queries = query_blocks[block_index]
        own_docs = doc_blocks[block_index]
        self_tile = tile_of(own_queries, own_docs)
        row_tiles = jnp.concatenate([self_tile, tile_of(own_queries, doc_blocks[first_partner]), tile_of(own_queries, doc_blocks[second_partner])], axis=1)
        col_tiles = jnp.concatenate([self_tile, tile_of(query_blocks[first_partner], own_docs), tile_of(query_blocks[second_partner], own_docs)], axis=0)
        return log_sum(row_tiles, 1), log_sum(col_tiles, 0)

    row_lse, column_lse = lax.map(statistics, block_ids)

    def gradients(block_index):
        first_partner = jnp.bitwise_xor(block_index, GRP_STRIDE)
        second_partner = jnp.bitwise_xor(block_index, DEV_STRIDE)
        own_queries = query_blocks[block_index]
        own_docs = doc_blocks[block_index]
        pair_row = pair_index[block_index]
        onehot = (pair_row[:, None] == jnp.arange(ROWS, dtype=jnp.int32)[None, :]).astype(jnp.float32)
        own_row = row_lse[block_index]
        own_col = column_lse[block_index]
        self_tile = tile_of(own_queries, own_docs)
        self_grad = (grad_tile(self_tile, own_row, own_col) - 2.0 * onehot).astype(jnp.bfloat16)
        query_sum = jnp.dot(self_grad, own_docs, preferred_element_type=jnp.float32)
        doc_sum = jnp.dot(self_grad.T, own_queries, preferred_element_type=jnp.float32)
        for partner in (first_partner, second_partner):
            far_docs = doc_blocks[partner]
            far_queries = query_blocks[partner]
            row_grad = grad_tile(tile_of(own_queries, far_docs), own_row, column_lse[partner]).astype(jnp.bfloat16)
            query_sum = query_sum + jnp.dot(row_grad, far_docs, preferred_element_type=jnp.float32)
            col_grad = grad_tile(tile_of(far_queries, own_docs), row_lse[partner], own_col).astype(jnp.bfloat16)
            doc_sum = doc_sum + rounded_share(jnp.dot(col_grad.T, far_queries, preferred_element_type=jnp.float32))
        positive_rows = jnp.sum(onehot * self_tile, axis=1)
        positive_columns = jnp.sum(onehot * self_tile, axis=0)
        return ((logit_scale * query_sum).astype(jnp.bfloat16), (logit_scale * doc_sum).astype(jnp.bfloat16), own_row - positive_rows, own_col - positive_columns)

    query_grad, doc_grad, row_loss, column_loss = lax.map(gradients, block_ids)
    return (query_grad.reshape(TOTAL, D), doc_grad.reshape(TOTAL, D), row_loss.reshape(TOTAL), column_loss.reshape(TOTAL))
```

```python
import jax
import jax.numpy as jnp
from jax import lax
from jax.experimental import pallas as pl
from jax.experimental.pallas import tpu as pltpu
from jax.sharding import PartitionSpec as P

logit_scale = 20.0
MESH = pl.DeviceIdType.MESH
ROWS = 512
D = 4096
K_CHUNK = 128
K_COUNT = ROWS // K_CHUNK
P_CHUNK = 64
P_COUNT = ROWS // P_CHUNK
WIDE = 512


def tile_into(out, left, right, first, count, step):
    @pl.loop(0, count)
    def _(i):
        at = pl.multiple_of(first + i * step, step)
        out[:, pl.ds(at, step)] = logit_scale * lax.dot_general(
            left[...],
            right[pl.ds(at, step), :],
            (((1,), (1,)), ((), ())),
            preferred_element_type=jnp.float32,
        )


def dot(a, b):
    return jnp.dot(a, b, preferred_element_type=jnp.float32)


def column_partial(tiles):
    top = tiles[0][...].max(axis=0, keepdims=True)
    for t in tiles[1:]:
        top = jnp.maximum(top, t[...].max(axis=0, keepdims=True))
    total = jnp.exp(tiles[0][...] - top).sum(axis=0, keepdims=True)
    for t in tiles[1:]:
        total = total + jnp.exp(t[...] - top).sum(axis=0, keepdims=True)
    return top, total


def row_partial(tiles):
    top = tiles[0][...].max(axis=1, keepdims=True)
    for t in tiles[1:]:
        top = jnp.maximum(top, t[...].max(axis=1, keepdims=True))
    total = jnp.exp(tiles[0][...] - top).sum(axis=1, keepdims=True)
    for t in tiles[1:]:
        total = total + jnp.exp(t[...] - top).sum(axis=1, keepdims=True)
    return top, total


def exchange(
    q_hbm, k_hbm, pair_ref, dq, dk, loss,
    q, k, q_core, k_core, k_far, share_out, share_in, acc,
    s_own, s_right, s_left, s_far,
    g_own, g_right, g_far, gt_own, gt_left, gt_far,
    row_top, row_sum, row_out, row_in, part_out, part_in,
    back_out, back_in, col_out, col_in,
    local_sem, doc_send, doc_recv, core_send, core_recv, stat_send, stat_recv,
    share_send, share_recv,
):
    g = lax.axis_index("grp")
    d = lax.axis_index("dev")
    core = lax.rem(g, 2)
    half = lax.axis_size("dev") // 2
    core_partner = (g + 1 - 2 * core, d)
    far_partner = (g, lax.rem(d + half, 2 * half))

    barrier = pltpu.get_barrier_semaphore()
    for other in (core_partner, far_partner):
        pl.semaphore_signal(barrier, inc=1, device_id=other, device_id_type=MESH)
    pl.semaphore_wait(barrier, 2)

    def remote(src, dst, send, recv, to):
        return pltpu.make_async_remote_copy(
            src_ref=src, dst_ref=dst, send_sem=send, recv_sem=recv,
            device_id=to, device_id_type=MESH,
        )

    def doc_copy(i):
        rows = pl.ds(i * K_CHUNK, K_CHUNK)
        return remote(k_hbm.at[rows], k_far.at[rows], doc_send.at[i], doc_recv.at[i], far_partner)

    def share_copy(i):
        rows = pl.ds(pl.multiple_of(i * P_CHUNK, P_CHUNK), P_CHUNK)
        return remote(
            share_out.at[rows], share_in.at[rows], share_send.at[i], share_recv.at[i], far_partner
        )

    @pl.when(core == 0)
    def _():
        for i in range(K_COUNT):
            doc_copy(i).start()

    k_move = remote(k_hbm, k_core, core_send.at[0], core_recv.at[0], core_partner)
    q_move = remote(q_hbm, q_core, core_send.at[1], core_recv.at[1], core_partner)
    q_load = pltpu.make_async_copy(q_hbm, q, local_sem.at[0])
    k_load = pltpu.make_async_copy(k_hbm, k, local_sem.at[1])
    q_load.start()
    k_load.start()
    k_move.start()
    q_move.start()
    q_load.wait()
    k_load.wait()
    tile_into(s_own, q, k, 0, 2, 256)
    k_move.wait_recv()
    tile_into(s_right, q, k_core, 0, 2, 256)
    q_move.wait_recv()
    tile_into(s_left, q_core, k, 0, 2, 256)

    top, total = column_partial([s_own, s_left])
    part_out[0:1, :] = top
    part_out[1:2, :] = total
    part_move = remote(part_out, part_in, stat_send.at[0], stat_recv.at[0], far_partner)
    part_move.start()

    @pl.when(core == 1)
    def _():
        for i in range(K_COUNT):
            doc_copy(i).start()

    top, total = row_partial([s_own, s_right])
    row_top[...] = jnp.broadcast_to(top, row_top.shape)
    row_sum[...] = jnp.broadcast_to(total, row_sum.shape)

    for i in range(K_COUNT):
        doc_copy(i).wait_recv()
        tile_into(s_far, q, k_far, i * K_CHUNK, 1, K_CHUNK)

    far_top, far_total = row_partial([s_far])
    near_top = row_top[:, 0:1]
    top = jnp.maximum(near_top, far_top)
    row_lse = top + jnp.log(
        row_sum[:, 0:1] * jnp.exp(near_top - top) + far_total * jnp.exp(far_top - top)
    )
    far_top, far_total = column_partial([s_far])
    part_move.wait_recv()
    near_top = part_in[0:1, :]
    top = jnp.maximum(near_top, far_top)
    far_lse = top + jnp.log(
        part_in[1:2, :] * jnp.exp(near_top - top) + far_total * jnp.exp(far_top - top)
    )
    back_out[0:1, :] = far_lse
    back_move = remote(back_out, back_in, stat_send.at[1], stat_recv.at[1], far_partner)
    back_move.start()
    weights = jnp.exp(s_far[...] - row_lse) + jnp.exp(s_far[...] - far_lse)
    g_far[...] = weights.astype(jnp.bfloat16)
    gt_far[...] = weights.T.astype(jnp.bfloat16)

    @pl.loop(0, P_COUNT)
    def _(i):
        rows = pl.ds(pl.multiple_of(i * P_CHUNK, P_CHUNK), P_CHUNK)
        share_out[rows, :] = dot(gt_far[rows, :], q[...]).astype(jnp.bfloat16)
        share_copy(i).start()

    row_out[...] = jnp.broadcast_to(row_lse, row_out.shape)
    row_move = remote(row_out, row_in, stat_send.at[2], stat_recv.at[2], core_partner)
    row_move.start()
    back_move.wait_recv()
    col_out[0:1, :] = back_in[0:1, :]
    col_move = remote(col_out, col_in, stat_send.at[3], stat_recv.at[3], core_partner)
    col_move.start()
    column_lse = back_in[0:1, :]

    row_lse = row_out[:, 0:1]
    pair = jnp.broadcast_to(pair_ref[...].astype(jnp.float32), (128, ROWS)).T[:, 0:1]
    places = lax.broadcasted_iota(jnp.int32, (ROWS, ROWS), 1)
    onehot = (pair.astype(jnp.int32) == places).astype(jnp.float32)
    own = s_own[...]
    weights = jnp.exp(own - row_lse) + jnp.exp(own - column_lse) - 2.0 * onehot
    g_own[...] = weights.astype(jnp.bfloat16)
    gt_own[...] = weights.T.astype(jnp.bfloat16)
    positive = onehot * own
    row_loss = row_lse - positive.sum(axis=1, keepdims=True)
    loss[0:1, :] = jnp.broadcast_to(row_loss, (ROWS, 128)).T[0:1, :]
    loss[1:2, :] = column_lse - positive.sum(axis=0, keepdims=True)

    row_move.wait_recv()
    col_move.wait_recv()
    right = s_right[...]
    g_right[...] = (jnp.exp(right - row_lse) + jnp.exp(right - col_in[0:1, :])).astype(jnp.bfloat16)
    left = s_left[...]
    weights = jnp.exp(left - row_in[:, 0:1]) + jnp.exp(left - column_lse)
    gt_left[...] = weights.T.astype(jnp.bfloat16)

    @pl.loop(0, D // WIDE)
    def _(i):
        at = pl.ds(pl.multiple_of(i * WIDE, WIDE), WIDE)
        total = dot(g_own[...], k[:, at]) + dot(g_right[...], k_core[:, at])
        total = total + dot(g_far[...], k_far[:, at])
        dq[:, at] = (logit_scale * total).astype(jnp.bfloat16)
        acc[:, at] = dot(gt_own[...], q[:, at]) + dot(gt_left[...], q_core[:, at])

    @pl.loop(0, P_COUNT)
    def _(i):
        share_copy(i).wait_recv()
        rows = pl.ds(pl.multiple_of(i * P_CHUNK, P_CHUNK), P_CHUNK)
        total = acc[rows, :] + share_in[rows, :].astype(jnp.float32)
        dk[rows, :] = (logit_scale * total).astype(jnp.bfloat16)

    for i in range(K_COUNT):
        doc_copy(i).wait_send()

    @pl.loop(0, P_COUNT)
    def _(i):
        share_copy(i).wait_send()

    for move in (k_move, q_move, part_move, back_move, row_move, col_move):
        move.wait_send()


def finish(dq_in, dk_in, loss_in, dq, dk, row_loss, column_loss, sem):
    first = pltpu.make_async_copy(dq_in, dq, sem.at[0])
    second = pltpu.make_async_copy(dk_in, dk, sem.at[1])
    first.start()
    second.start()
    row_loss[...] = loss_in[0, :]
    column_loss[...] = loss_in[1, :]
    first.wait()
    second.wait()


def shards(queries, documents, pair_index):
    vmem = pl.BlockSpec(memory_space=pltpu.VMEM)
    anywhere = pl.BlockSpec(memory_space=pl.ANY)
    block = lambda *shape, dtype=jnp.bfloat16: pltpu.VMEM(shape, dtype)
    f32 = jnp.float32
    big = jax.ShapeDtypeStruct((ROWS, D), jnp.bfloat16)
    dq, dk, loss = pl.pallas_call(
        exchange,
        out_shape=(big, big, jax.ShapeDtypeStruct((8, ROWS), f32)),
        in_specs=[anywhere, anywhere, vmem],
        out_specs=(vmem, vmem, vmem),
        scratch_shapes=[block(ROWS, D) for _ in range(7)]
        + [block(ROWS, D, dtype=f32)]
        + [block(ROWS, ROWS, dtype=f32) for _ in range(4)]
        + [block(ROWS, ROWS) for _ in range(6)]
        + [block(ROWS, 128, dtype=f32) for _ in range(4)]
        + [block(8, ROWS, dtype=f32) for _ in range(6)]
        + [
            pltpu.SemaphoreType.DMA((n,))
            for n in (2, K_COUNT, K_COUNT, 2, 2, 4, 4, P_COUNT, P_COUNT)
        ],
        compiler_params=pltpu.CompilerParams(
            collective_id=0, has_side_effects=True, vmem_limit_bytes=60 << 20
        ),
        cost_estimate=pl.CostEstimate(
            flops=20 * ROWS * ROWS * D, bytes_accessed=16 * ROWS * D, transcendentals=8 * ROWS * ROWS
        ),
    )(queries, documents, pair_index)
    vector = jax.ShapeDtypeStruct((ROWS,), f32)
    return pl.pallas_call(
        finish,
        out_shape=(big, big, vector, vector),
        in_specs=[vmem, vmem, vmem],
        out_specs=(anywhere, anywhere, vmem, vmem),
        scratch_shapes=[pltpu.SemaphoreType.DMA((2,))],
        compiler_params=pltpu.CompilerParams(vmem_limit_bytes=16 << 20),
    )(dq, dk, loss)


def solution(mesh):
    rows = P(("grp", "dev"), None)
    flat = P(("grp", "dev"))
    return jax.shard_map(
        shards,
        mesh=mesh,
        in_specs=(rows, rows, rows),
        out_specs=(rows, rows, flat, flat),
        check_vma=False,
    )
```

```python
import jax
import jax.numpy as jnp
from jax import lax
from jax.experimental import pallas as pl
from jax.experimental.pallas import tpu as pltpu
from jax.sharding import PartitionSpec as P

logit_scale = 20.0
MESH = pl.DeviceIdType.MESH
ROWS = 512
D = 4096
K_CHUNK = 128
K_COUNT = ROWS // K_CHUNK
P_CHUNK = 128
LAST = 128
HEAD = ROWS - LAST
P_COUNT = HEAD // P_CHUNK
WIDE = 1024


def tile_into(out, left, right, first, count, step):
    @pl.loop(0, count)
    def _(i):
        at = pl.multiple_of(first + i * step, step)
        out[:, pl.ds(at, step)] = logit_scale * lax.dot_general(
            left[...],
            right[pl.ds(at, step), :],
            (((1,), (1,)), ((), ())),
            preferred_element_type=jnp.float32,
        )


def dot(a, b):
    return jnp.dot(a, b, preferred_element_type=jnp.float32)


def column_partial(tiles):
    top = tiles[0][...].max(axis=0, keepdims=True)
    for t in tiles[1:]:
        top = jnp.maximum(top, t[...].max(axis=0, keepdims=True))
    total = jnp.exp(tiles[0][...] - top).sum(axis=0, keepdims=True)
    for t in tiles[1:]:
        total = total + jnp.exp(t[...] - top).sum(axis=0, keepdims=True)
    return top, total


def row_partial(tiles):
    top = tiles[0][...].max(axis=1, keepdims=True)
    for t in tiles[1:]:
        top = jnp.maximum(top, t[...].max(axis=1, keepdims=True))
    total = jnp.exp(tiles[0][...] - top).sum(axis=1, keepdims=True)
    for t in tiles[1:]:
        total = total + jnp.exp(t[...] - top).sum(axis=1, keepdims=True)
    return top, total


def exchange(
    q_hbm, k_hbm, pair_ref, dq_hbm, dk_hbm, share_hbm, acc_hbm, loss,
    q, k, q_core, k_core, k_far, share_out, dq, share_in, dk, acc,
    s_own, s_right, s_left, s_far,
    g_own, g_right, g_far, gt_own, gt_left, gt_far,
    row_top, row_sum, row_out, row_in, part_out, part_in,
    back_out, back_in, col_out, col_in,
    local_sem, doc_send, doc_recv, core_send, core_recv, stat_send, stat_recv,
    share_send, share_recv, out_sem, dk_sem,
):
    g = lax.axis_index("grp")
    d = lax.axis_index("dev")
    core = lax.rem(g, 2)
    half = lax.axis_size("dev") // 2
    core_partner = (g + 1 - 2 * core, d)
    far_partner = (g, lax.rem(d + half, 2 * half))

    barrier = pltpu.get_barrier_semaphore()
    for other in (core_partner, far_partner):
        pl.semaphore_signal(barrier, inc=1, device_id=other, device_id_type=MESH)
    pl.semaphore_wait(barrier, 2)

    def remote(src, dst, send, recv, to):
        return pltpu.make_async_remote_copy(
            src_ref=src, dst_ref=dst, send_sem=send, recv_sem=recv,
            device_id=to, device_id_type=MESH,
        )

    def doc_copy(i):
        rows = pl.ds(i * K_CHUNK, K_CHUNK)
        return remote(k_hbm.at[rows], k_far.at[rows], doc_send.at[i], doc_recv.at[i], far_partner)

    def share_copy(i):
        rows = pl.ds(pl.multiple_of(i * P_CHUNK, P_CHUNK), P_CHUNK)
        return remote(
            share_out.at[rows], share_in.at[rows], share_send.at[i], share_recv.at[i], far_partner
        )

    @pl.when(core == 0)
    def _():
        for i in range(K_COUNT):
            doc_copy(i).start()

    k_move = remote(k_hbm, k_core, core_send.at[0], core_recv.at[0], core_partner)
    q_move = remote(q_hbm, q_core, core_send.at[1], core_recv.at[1], core_partner)
    q_load = pltpu.make_async_copy(q_hbm, q, local_sem.at[0])
    k_load = pltpu.make_async_copy(k_hbm, k, local_sem.at[1])
    q_load.start()
    k_load.start()
    k_move.start()
    q_move.start()
    q_load.wait()
    k_load.wait()
    tile_into(s_own, q, k, 0, 2, 256)
    k_move.wait_recv()
    tile_into(s_right, q, k_core, 0, 2, 256)
    q_move.wait_recv()
    @pl.when(core == 1)
    def _():
        for i in range(K_COUNT):
            doc_copy(i).start()

    tile_into(s_left, q_core, k, 0, 2, 256)

    top, total = column_partial([s_own, s_left])
    part_out[0:1, :] = top
    part_out[1:2, :] = total
    part_move = remote(part_out, part_in, stat_send.at[0], stat_recv.at[0], far_partner)
    part_move.start()

    top, total = row_partial([s_own, s_right])
    row_top[...] = jnp.broadcast_to(top, row_top.shape)
    row_sum[...] = jnp.broadcast_to(total, row_sum.shape)

    for i in range(K_COUNT):
        doc_copy(i).wait_recv()
        tile_into(s_far, q, k_far, i * K_CHUNK, 1, K_CHUNK)

    far_top, far_total = row_partial([s_far])
    near_top = row_top[:, 0:1]
    top = jnp.maximum(near_top, far_top)
    row_lse = top + jnp.log(
        row_sum[:, 0:1] * jnp.exp(near_top - top) + far_total * jnp.exp(far_top - top)
    )
    far_top, far_total = column_partial([s_far])
    part_move.wait_recv()
    near_top = part_in[0:1, :]
    top = jnp.maximum(near_top, far_top)
    far_lse = top + jnp.log(
        part_in[1:2, :] * jnp.exp(near_top - top) + far_total * jnp.exp(far_top - top)
    )
    back_out[0:1, :] = far_lse
    back_move = remote(back_out, back_in, stat_send.at[1], stat_recv.at[1], far_partner)
    back_move.start()
    weights = jnp.exp(s_far[...] - row_lse) + jnp.exp(s_far[...] - far_lse)
    g_far[...] = weights.astype(jnp.bfloat16)
    gt_far[...] = weights.T.astype(jnp.bfloat16)

    @pl.loop(0, P_COUNT)
    def _(i):
        rows = pl.ds(pl.multiple_of(i * P_CHUNK, P_CHUNK), P_CHUNK)
        share_out[rows, :] = dot(gt_far[rows, :], q[...]).astype(jnp.bfloat16)
        share_copy(i).start()

    tail = pl.ds(HEAD, LAST)
    share_out[tail, :] = dot(gt_far[tail, :], q[...]).astype(jnp.bfloat16)
    share_store = pltpu.make_async_copy(share_out.at[tail], share_hbm, out_sem.at[0])
    share_store.start()

    row_out[...] = jnp.broadcast_to(row_lse, row_out.shape)
    row_move = remote(row_out, row_in, stat_send.at[2], stat_recv.at[2], core_partner)
    row_move.start()
    back_move.wait_recv()
    col_out[0:1, :] = back_in[0:1, :]
    col_move = remote(col_out, col_in, stat_send.at[3], stat_recv.at[3], core_partner)
    col_move.start()
    column_lse = back_in[0:1, :]

    row_lse = row_out[:, 0:1]
    pair = jnp.broadcast_to(pair_ref[...].astype(jnp.float32), (128, ROWS)).T[:, 0:1]
    places = lax.broadcasted_iota(jnp.int32, (ROWS, ROWS), 1)
    onehot = (pair.astype(jnp.int32) == places).astype(jnp.float32)
    own = s_own[...]
    weights = jnp.exp(own - row_lse) + jnp.exp(own - column_lse) - 2.0 * onehot
    g_own[...] = weights.astype(jnp.bfloat16)
    gt_own[...] = weights.T.astype(jnp.bfloat16)
    positive = onehot * own
    row_loss = row_lse - positive.sum(axis=1, keepdims=True)
    loss[0:1, :] = jnp.broadcast_to(row_loss, (ROWS, 128)).T[0:1, :]
    loss[1:2, :] = column_lse - positive.sum(axis=0, keepdims=True)

    row_move.wait_recv()
    col_move.wait_recv()
    right = s_right[...]
    g_right[...] = (jnp.exp(right - row_lse) + jnp.exp(right - col_in[0:1, :])).astype(jnp.bfloat16)
    left = s_left[...]
    weights = jnp.exp(left - row_in[:, 0:1]) + jnp.exp(left - column_lse)
    gt_left[...] = weights.T.astype(jnp.bfloat16)

    @pl.loop(0, D // WIDE)
    def _(i):
        at = pl.ds(pl.multiple_of(i * WIDE, WIDE), WIDE)
        total = dot(g_own[...], k[:, at]) + dot(g_right[...], k_core[:, at])
        total = total + dot(g_far[...], k_far[:, at])
        dq[:, at] = (logit_scale * total).astype(jnp.bfloat16)
        acc[:, at] = dot(gt_own[...], q[:, at]) + dot(gt_left[...], q_core[:, at])

    dq_store = pltpu.make_async_copy(dq, dq_hbm, out_sem.at[1])
    dq_store.start()
    acc_store = pltpu.make_async_copy(acc.at[tail], acc_hbm, out_sem.at[2])
    acc_store.start()

    def dk_store(i):
        rows = pl.ds(pl.multiple_of(i * P_CHUNK, P_CHUNK), P_CHUNK)
        return pltpu.make_async_copy(dk.at[rows], dk_hbm.at[rows], dk_sem.at[i])

    @pl.loop(0, P_COUNT)
    def _(i):
        share_copy(i).wait_recv()
        rows = pl.ds(pl.multiple_of(i * P_CHUNK, P_CHUNK), P_CHUNK)
        total = acc[rows, :] + share_in[rows, :].astype(jnp.float32)
        dk[rows, :] = (logit_scale * total).astype(jnp.bfloat16)
        dk_store(i).start()

    for i in range(K_COUNT):
        doc_copy(i).wait_send()

    @pl.loop(0, P_COUNT)
    def _(i):
        share_copy(i).wait_send()
        dk_store(i).wait()

    for store in (share_store, dq_store, acc_store):
        store.wait()
    for move in (k_move, q_move, part_move, back_move, row_move, col_move):
        move.wait_send()


def settle(dq_in, dk_in, loss_in, dq, dk, row_loss, column_loss, sem):
    first = pltpu.make_async_copy(dq_in, dq, sem.at[0])
    second = pltpu.make_async_copy(dk_in, dk.at[pl.ds(0, HEAD)], sem.at[1])
    first.start()
    second.start()
    row_loss[...] = loss_in[0, :]
    column_loss[...] = loss_in[1, :]
    first.wait()
    second.wait()


def finish(acc, share, dk_in, dk, out, sem):
    total = acc[...] + share[...].astype(jnp.float32)
    out[...] = (logit_scale * total).astype(jnp.bfloat16)
    store = pltpu.make_async_copy(out, dk.at[pl.ds(HEAD, LAST)], sem)
    store.start()
    store.wait()


def shards(queries, documents, pair_index):
    vmem = pl.BlockSpec(memory_space=pltpu.VMEM)
    anywhere = pl.BlockSpec(memory_space=pl.ANY)
    f32, bf16 = jnp.float32, jnp.bfloat16
    block = lambda *shape, dtype=bf16: pltpu.VMEM(shape, dtype)
    out = jax.ShapeDtypeStruct
    big = out((ROWS, D), bf16)
    dq, dk_head, share_tail, acc_tail, loss = pl.pallas_call(
        exchange,
        out_shape=(big, out((HEAD, D), bf16), out((LAST, D), bf16), out((LAST, D), f32), out((8, ROWS), f32)),
        in_specs=[anywhere, anywhere, vmem],
        out_specs=(anywhere, anywhere, anywhere, anywhere, vmem),
        scratch_shapes=[block(ROWS, D) for _ in range(7)]
        + [block(HEAD, D) for _ in range(2)]
        + [block(ROWS, D, dtype=f32)]
        + [block(ROWS, ROWS, dtype=f32) for _ in range(4)]
        + [block(ROWS, ROWS) for _ in range(6)]
        + [block(ROWS, 128, dtype=f32) for _ in range(4)]
        + [block(8, ROWS, dtype=f32) for _ in range(6)]
        + [
            pltpu.SemaphoreType.DMA((n,))
            for n in (2, K_COUNT, K_COUNT, 2, 2, 4, 4, P_COUNT, P_COUNT, 3, P_COUNT)
        ],
        compiler_params=pltpu.CompilerParams(
            collective_id=0, has_side_effects=True, vmem_limit_bytes=60 << 20
        ),
        cost_estimate=pl.CostEstimate(
            flops=20 * ROWS * ROWS * D, bytes_accessed=16 * ROWS * D, transcendentals=8 * ROWS * ROWS
        ),
    )(queries, documents, pair_index)
    grp_count, dev_count = lax.axis_size("grp"), lax.axis_size("dev")
    route = [(i, i ^ (dev_count // 2)) for i in range(grp_count * dev_count)]
    share = lax.ppermute(share_tail, ("grp", "dev"), route)
    vector = out((ROWS,), f32)
    dq, dk, row_loss, column_loss = pl.pallas_call(
        settle,
        out_shape=(big, big, vector, vector),
        in_specs=[anywhere, anywhere, vmem],
        out_specs=(anywhere, anywhere, vmem, vmem),
        scratch_shapes=[pltpu.SemaphoreType.DMA((2,))],
        compiler_params=pltpu.CompilerParams(vmem_limit_bytes=16 << 20),
        cost_estimate=pl.CostEstimate(flops=0, bytes_accessed=8 * ROWS * D, transcendentals=0),
    )(dq, dk_head, loss)
    dk = pl.pallas_call(
        finish,
        out_shape=big,
        in_specs=[vmem, vmem, anywhere],
        out_specs=anywhere,
        input_output_aliases={2: 0},
        scratch_shapes=[block(LAST, D), pltpu.SemaphoreType.DMA],
        compiler_params=pltpu.CompilerParams(vmem_limit_bytes=16 << 20),
        cost_estimate=pl.CostEstimate(flops=2 * LAST * D, bytes_accessed=8 * LAST * D, transcendentals=0),
    )(acc_tail, share, dk)
    return dq, dk, row_loss, column_loss


def solution(mesh):
    rows = P(("grp", "dev"), None)
    flat = P(("grp", "dev"))
    return jax.shard_map(
        shards,
        mesh=mesh,
        in_specs=(rows, rows, rows),
        out_specs=(rows, rows, flat, flat),
        check_vma=False,
    )
```

```python
import jax
import jax.numpy as jnp
from jax import lax
from jax.experimental import pallas as pl
from jax.experimental.pallas import tpu as pltpu
from jax.sharding import PartitionSpec as P

logit_scale = 20.0
MESH = pl.DeviceIdType.MESH
ROWS = 512
D = 4096
K_CHUNK = 256
K_COUNT = ROWS // K_CHUNK
P_CHUNK = 128
LAST = 128
HEAD = ROWS - LAST
P_COUNT = HEAD // P_CHUNK
WIDE = 1024
SLAB = 64


def tile_into(out, left, right, first, count, step):
    @pl.loop(0, count)
    def _(i):
        at = pl.multiple_of(first + i * step, step)
        out[:, pl.ds(at, step)] = logit_scale * lax.dot_general(
            left[...],
            right[pl.ds(at, step), :],
            (((1,), (1,)), ((), ())),
            preferred_element_type=jnp.float32,
        )


def dot(a, b):
    return jnp.dot(a, b, preferred_element_type=jnp.float32)


def column_partial(tiles):
    top = tiles[0][...].max(axis=0, keepdims=True)
    for t in tiles[1:]:
        top = jnp.maximum(top, t[...].max(axis=0, keepdims=True))
    total = jnp.exp(tiles[0][...] - top).sum(axis=0, keepdims=True)
    for t in tiles[1:]:
        total = total + jnp.exp(t[...] - top).sum(axis=0, keepdims=True)
    return top, total


def row_partial(tiles):
    top = tiles[0][...].max(axis=1, keepdims=True)
    for t in tiles[1:]:
        top = jnp.maximum(top, t[...].max(axis=1, keepdims=True))
    total = jnp.exp(tiles[0][...] - top).sum(axis=1, keepdims=True)
    for t in tiles[1:]:
        total = total + jnp.exp(t[...] - top).sum(axis=1, keepdims=True)
    return top, total


def exchange(
    q_hbm, k_hbm, pair_hbm, dq_hbm, dk_hbm, share_hbm, acc_hbm, loss_hbm,
    q, k, q_core, k_core, k_far, share_out, dq, share_in, dk, acc,
    s_own, s_right, s_left, s_far,
    g_own, g_right, g_far, gt_own, gt_left, gt_far,
    row_top, row_sum, row_out, row_in, part_out, part_in,
    back_out, back_in, col_out, col_in, loss, pair_ref,
    local_sem, doc_send, doc_recv, core_send, core_recv, stat_send, stat_recv,
    share_send, share_recv, out_sem, dk_sem,
):
    g = lax.axis_index("grp")
    d = lax.axis_index("dev")
    core = lax.rem(g, 2)
    half = lax.axis_size("dev") // 2
    core_partner = (g + 1 - 2 * core, d)
    far_partner = (g, lax.rem(d + half, 2 * half))

    barrier = pltpu.get_barrier_semaphore()
    for other in (core_partner, far_partner):
        pl.semaphore_signal(barrier, inc=1, device_id=other, device_id_type=MESH)
    pl.semaphore_wait(barrier, 2)

    def remote(src, dst, send, recv, to):
        return pltpu.make_async_remote_copy(
            src_ref=src, dst_ref=dst, send_sem=send, recv_sem=recv,
            device_id=to, device_id_type=MESH,
        )

    def doc_copy(i):
        rows = pl.ds(i * K_CHUNK, K_CHUNK)
        return remote(k_hbm.at[rows], k_far.at[rows], doc_send.at[i], doc_recv.at[i], far_partner)

    def share_copy(i):
        rows = pl.ds(pl.multiple_of(i * P_CHUNK, P_CHUNK), P_CHUNK)
        return remote(
            share_out.at[rows], share_in.at[rows], share_send.at[i], share_recv.at[i], far_partner
        )

    @pl.when(core == 0)
    def _():
        for i in range(K_COUNT):
            doc_copy(i).start()

    k_move = remote(k_hbm, k_core, core_send.at[0], core_recv.at[0], core_partner)
    q_move = remote(q_hbm, q_core, core_send.at[1], core_recv.at[1], core_partner)
    q_load = pltpu.make_async_copy(q_hbm, q, local_sem.at[0])
    k_load = pltpu.make_async_copy(k_hbm, k, local_sem.at[1])
    pair_load = pltpu.make_async_copy(pair_hbm, pair_ref, local_sem.at[2])
    q_load.start()
    k_load.start()
    pair_load.start()
    k_move.start()
    q_move.start()
    q_load.wait()
    k_load.wait()
    pair_load.wait()
    tile_into(s_own, q, k, 0, 2, 256)
    k_move.wait_recv()
    tile_into(s_right, q, k_core, 0, 2, 256)
    q_move.wait_recv()
    @pl.when(core == 1)
    def _():
        for i in range(K_COUNT):
            doc_copy(i).start()

    tile_into(s_left, q_core, k, 0, 2, 256)

    top, total = column_partial([s_own, s_left])
    part_out[0:1, :] = top
    part_out[1:2, :] = total
    part_move = remote(part_out, part_in, stat_send.at[0], stat_recv.at[0], far_partner)
    part_move.start()

    top, total = row_partial([s_own, s_right])
    row_top[...] = jnp.broadcast_to(top, row_top.shape)
    row_sum[...] = jnp.broadcast_to(total, row_sum.shape)

    for i in range(K_COUNT):
        doc_copy(i).wait_recv()
        tile_into(s_far, q, k_far, i * K_CHUNK, 1, K_CHUNK)

    far_top, far_total = row_partial([s_far])
    near_top = row_top[:, 0:1]
    top = jnp.maximum(near_top, far_top)
    row_lse = top + jnp.log(
        row_sum[:, 0:1] * jnp.exp(near_top - top) + far_total * jnp.exp(far_top - top)
    )
    far_top, far_total = column_partial([s_far])
    part_move.wait_recv()
    near_top = part_in[0:1, :]
    top = jnp.maximum(near_top, far_top)
    far_lse = top + jnp.log(
        part_in[1:2, :] * jnp.exp(near_top - top) + far_total * jnp.exp(far_top - top)
    )
    back_out[0:1, :] = far_lse
    back_move = remote(back_out, back_in, stat_send.at[1], stat_recv.at[1], far_partner)
    back_move.start()
    weights = jnp.exp(s_far[...] - row_lse) + jnp.exp(s_far[...] - far_lse)
    g_far[...] = weights.astype(jnp.bfloat16)
    gt_far[...] = weights.T.astype(jnp.bfloat16)

    @pl.loop(0, P_COUNT)
    def _(i):
        rows = pl.ds(pl.multiple_of(i * P_CHUNK, P_CHUNK), P_CHUNK)
        share_out[rows, :] = dot(gt_far[rows, :], q[...]).astype(jnp.bfloat16)
        share_copy(i).start()

    tail = pl.ds(HEAD, LAST)
    share_out[tail, :] = dot(gt_far[tail, :], q[...]).astype(jnp.bfloat16)
    share_store = pltpu.make_async_copy(share_out.at[tail], share_hbm, out_sem.at[0])
    share_store.start()

    row_out[...] = jnp.broadcast_to(row_lse, row_out.shape)
    row_move = remote(row_out, row_in, stat_send.at[2], stat_recv.at[2], core_partner)
    row_move.start()
    back_move.wait_recv()
    col_out[0:1, :] = back_in[0:1, :]
    col_move = remote(col_out, col_in, stat_send.at[3], stat_recv.at[3], core_partner)
    col_move.start()
    column_lse = back_in[0:1, :]

    row_lse = row_out[:, 0:1]
    pair = jnp.broadcast_to(pair_ref[...].astype(jnp.float32), (128, ROWS)).T[:, 0:1]
    places = lax.broadcasted_iota(jnp.int32, (ROWS, ROWS), 1)
    onehot = (pair.astype(jnp.int32) == places).astype(jnp.float32)
    own = s_own[...]
    weights = jnp.exp(own - row_lse) + jnp.exp(own - column_lse) - 2.0 * onehot
    g_own[...] = weights.astype(jnp.bfloat16)
    gt_own[...] = weights.T.astype(jnp.bfloat16)
    positive = onehot * own
    row_loss = row_lse - positive.sum(axis=1, keepdims=True)
    loss[0:1, :] = jnp.broadcast_to(row_loss, (ROWS, 128)).T[0:1, :]
    loss[1:2, :] = column_lse - positive.sum(axis=0, keepdims=True)

    loss_store = pltpu.make_async_copy(loss, loss_hbm, out_sem.at[3])
    loss_store.start()

    row_move.wait_recv()
    col_move.wait_recv()
    right = s_right[...]
    g_right[...] = (jnp.exp(right - row_lse) + jnp.exp(right - col_in[0:1, :])).astype(jnp.bfloat16)
    left = s_left[...]
    weights = jnp.exp(left - row_in[:, 0:1]) + jnp.exp(left - column_lse)
    gt_left[...] = weights.T.astype(jnp.bfloat16)

    @pl.loop(0, D // WIDE)
    def _(i):
        at = pl.ds(pl.multiple_of(i * WIDE, WIDE), WIDE)
        total = dot(g_own[...], k[:, at]) + dot(g_right[...], k_core[:, at])
        total = total + dot(g_far[...], k_far[:, at])
        dq[:, at] = (logit_scale * total).astype(jnp.bfloat16)
        acc[:, at] = dot(gt_own[...], q[:, at]) + dot(gt_left[...], q_core[:, at])

    dq_store = pltpu.make_async_copy(dq, dq_hbm, out_sem.at[1])
    dq_store.start()
    acc_store = pltpu.make_async_copy(acc.at[tail], acc_hbm, out_sem.at[2])
    acc_store.start()

    def dk_store(i):
        rows = pl.ds(pl.multiple_of(i * P_CHUNK, P_CHUNK), P_CHUNK)
        return pltpu.make_async_copy(dk.at[rows], dk_hbm.at[rows], dk_sem.at[i])

    @pl.loop(0, P_COUNT)
    def _(i):
        share_copy(i).wait_recv()
        rows = pl.ds(pl.multiple_of(i * P_CHUNK, P_CHUNK), P_CHUNK)
        total = acc[rows, :] + share_in[rows, :].astype(jnp.float32)
        dk[rows, :] = (logit_scale * total).astype(jnp.bfloat16)
        dk_store(i).start()

    for i in range(K_COUNT):
        doc_copy(i).wait_send()

    @pl.loop(0, P_COUNT)
    def _(i):
        share_copy(i).wait_send()
        dk_store(i).wait()

    for store in (share_store, dq_store, acc_store, loss_store):
        store.wait()
    for move in (k_move, q_move, part_move, back_move, row_move, col_move):
        move.wait_send()


def settle(dq_in, dk_in, loss_in, dq, dk, row_loss, column_loss, held, loss, load_sem, store_sem, sem):
    parts = [(dq_in, dq, r) for r in range(0, ROWS, SLAB)] + [(dk_in, dk, r) for r in range(0, HEAD, SLAB)]

    def load(i):
        src, _, r = parts[i]
        return pltpu.make_async_copy(src.at[pl.ds(r, SLAB)], held.at[i], load_sem.at[i])

    def store(i):
        _, dst, r = parts[i]
        return pltpu.make_async_copy(held.at[i], dst.at[pl.ds(r, SLAB)], store_sem.at[i])

    loss_load = pltpu.make_async_copy(loss_in, loss, sem)
    loss_load.start()
    for i in range(len(parts)):
        load(i).start()
    loss_load.wait()
    row_loss[...] = loss[0, :]
    column_loss[...] = loss[1, :]
    for i in range(len(parts)):
        load(i).wait()
        store(i).start()
    for i in range(len(parts)):
        store(i).wait()


def finish(acc, share, dk_in, dk, out, sem):
    stores = []
    for r in range(0, LAST, LAST // 4):
        part = pl.ds(r, LAST // 4)
        total = acc[part, :] + share[part, :].astype(jnp.float32)
        out[part, :] = (logit_scale * total).astype(jnp.bfloat16)
        stores.append(pltpu.make_async_copy(out.at[part], dk.at[pl.ds(HEAD + r, LAST // 4)], sem.at[len(stores)]))
        stores[-1].start()
    for store in stores:
        store.wait()


def shards(queries, documents, pair_index):
    vmem = pl.BlockSpec(memory_space=pltpu.VMEM)
    anywhere = pl.BlockSpec(memory_space=pl.ANY)
    f32, bf16 = jnp.float32, jnp.bfloat16
    block = lambda *shape, dtype=bf16: pltpu.VMEM(shape, dtype)
    out = jax.ShapeDtypeStruct
    big = out((ROWS, D), bf16)
    dq, dk_head, share_tail, acc_tail, loss = pl.pallas_call(
        exchange,
        out_shape=(big, out((HEAD, D), bf16), out((LAST, D), bf16), out((LAST, D), f32), out((8, ROWS), f32)),
        in_specs=[anywhere, anywhere, anywhere],
        out_specs=(anywhere, anywhere, anywhere, anywhere, anywhere),
        scratch_shapes=[block(ROWS, D) for _ in range(7)]
        + [block(HEAD, D) for _ in range(2)]
        + [block(ROWS, D, dtype=f32)]
        + [block(ROWS, ROWS, dtype=f32) for _ in range(4)]
        + [block(ROWS, ROWS) for _ in range(6)]
        + [block(ROWS, 128, dtype=f32) for _ in range(4)]
        + [block(8, ROWS, dtype=f32) for _ in range(7)]
        + [block(1, ROWS, dtype=jnp.int32)]
        + [
            pltpu.SemaphoreType.DMA((n,))
            for n in (3, K_COUNT, K_COUNT, 2, 2, 4, 4, P_COUNT, P_COUNT, 4, P_COUNT)
        ],
        compiler_params=pltpu.CompilerParams(
            collective_id=0, has_side_effects=True, vmem_limit_bytes=60 << 20
        ),
        cost_estimate=pl.CostEstimate(
            flops=20 * ROWS * ROWS * D, bytes_accessed=16 * ROWS * D, transcendentals=8 * ROWS * ROWS
        ),
    )(queries, documents, pair_index)
    grp_count, dev_count = lax.axis_size("grp"), lax.axis_size("dev")
    route = [(i, i ^ (dev_count // 2)) for i in range(grp_count * dev_count)]
    share = lax.ppermute(share_tail, ("grp", "dev"), route)
    vector = out((ROWS,), f32)
    dq, dk, row_loss, column_loss = pl.pallas_call(
        settle,
        out_shape=(big, big, vector, vector),
        in_specs=[anywhere, anywhere, anywhere],
        out_specs=(anywhere, anywhere, vmem, vmem),
        scratch_shapes=[
            block((ROWS + HEAD) // SLAB, SLAB, D),
            block(8, ROWS, dtype=f32),
            pltpu.SemaphoreType.DMA(((ROWS + HEAD) // SLAB,)),
            pltpu.SemaphoreType.DMA(((ROWS + HEAD) // SLAB,)),
            pltpu.SemaphoreType.DMA,
        ],
        compiler_params=pltpu.CompilerParams(vmem_limit_bytes=60 << 20),
        cost_estimate=pl.CostEstimate(flops=0, bytes_accessed=8 * ROWS * D, transcendentals=0),
    )(dq, dk_head, loss)
    dk = pl.pallas_call(
        finish,
        out_shape=big,
        in_specs=[vmem, vmem, anywhere],
        out_specs=anywhere,
        input_output_aliases={2: 0},
        scratch_shapes=[block(LAST, D), pltpu.SemaphoreType.DMA((4,))],
        compiler_params=pltpu.CompilerParams(vmem_limit_bytes=16 << 20),
        cost_estimate=pl.CostEstimate(flops=2 * LAST * D, bytes_accessed=8 * LAST * D, transcendentals=0),
    )(acc_tail, share, dk)
    return dq, dk, row_loss, column_loss


def solution(mesh):
    rows = P(("grp", "dev"), None)
    flat = P(("grp", "dev"))
    return jax.shard_map(
        shards,
        mesh=mesh,
        in_specs=(rows, rows, rows),
        out_specs=(rows, rows, flat, flat),
        check_vma=False,
    )
```

```python
import jax
import jax.numpy as jnp
from jax import lax
from jax.experimental import pallas as pl
from jax.experimental.pallas import tpu as pltpu
from jax.sharding import PartitionSpec as P

logit_scale = 20.0
MESH = pl.DeviceIdType.MESH
ROWS = 512
D = 4096
K_CHUNK = 256
K_COUNT = D // K_CHUNK
AHEAD = 3
P_CHUNK = 128
LAST = 128
HEAD = ROWS - LAST
P_COUNT = HEAD // P_CHUNK
WIDE = 256
SLAB = 64


def tile_into(out, left, right, first, count, step):
    @pl.loop(0, count)
    def _(i):
        at = pl.multiple_of(first + i * step, step)
        out[:, pl.ds(at, step)] = logit_scale * lax.dot_general(
            left[...],
            right[pl.ds(at, step), :],
            (((1,), (1,)), ((), ())),
            preferred_element_type=jnp.float32,
        )


def dot(a, b):
    return jnp.dot(a, b, preferred_element_type=jnp.float32)


def column_partial(tiles):
    top = tiles[0][...].max(axis=0, keepdims=True)
    for t in tiles[1:]:
        top = jnp.maximum(top, t[...].max(axis=0, keepdims=True))
    total = jnp.exp(tiles[0][...] - top).sum(axis=0, keepdims=True)
    for t in tiles[1:]:
        total = total + jnp.exp(t[...] - top).sum(axis=0, keepdims=True)
    return top, total


def row_partial(tiles):
    top = tiles[0][...].max(axis=1, keepdims=True)
    for t in tiles[1:]:
        top = jnp.maximum(top, t[...].max(axis=1, keepdims=True))
    total = jnp.exp(tiles[0][...] - top).sum(axis=1, keepdims=True)
    for t in tiles[1:]:
        total = total + jnp.exp(t[...] - top).sum(axis=1, keepdims=True)
    return top, total


def exchange(
    q_hbm, k_hbm, pair_hbm, dq_hbm, dk_hbm, share_hbm, acc_hbm, loss_hbm,
    q, k, q_core, k_core, k_far, share_out, dq, share_in, dk, acc,
    s_own, s_right, s_left, s_far,
    g_own, g_right, g_far, gt_own, gt_left, gt_far,
    row_top, row_sum, row_out, row_in, part_out, part_in,
    back_out, back_in, col_out, col_in, loss, pair_ref,
    local_sem, doc_send, doc_recv, core_send, core_recv, stat_send, stat_recv,
    share_send, share_recv, out_sem, dk_sem, go_sem,
):
    g = lax.axis_index("grp")
    d = lax.axis_index("dev")
    core = lax.rem(g, 2)
    half = lax.axis_size("dev") // 2
    core_partner = (g + 1 - 2 * core, d)
    far_partner = (g, lax.rem(d + half, 2 * half))

    barrier = pltpu.get_barrier_semaphore()
    for other in (core_partner, far_partner):
        pl.semaphore_signal(barrier, inc=1, device_id=other, device_id_type=MESH)
    pl.semaphore_wait(barrier, 2)

    def remote(src, dst, send, recv, to):
        return pltpu.make_async_remote_copy(
            src_ref=src, dst_ref=dst, send_sem=send, recv_sem=recv,
            device_id=to, device_id_type=MESH,
        )

    def doc_copy(i):
        part = pl.ds(pl.multiple_of(i * K_CHUNK, K_CHUNK), K_CHUNK)
        return remote(
            k_hbm.at[:, part], k_far.at[:, part], doc_send.at[i], doc_recv.at[i], far_partner
        )

    def share_copy(i):
        rows = pl.ds(pl.multiple_of(i * P_CHUNK, P_CHUNK), P_CHUNK)
        return remote(
            share_out.at[rows], share_in.at[rows], share_send.at[i], share_recv.at[i], far_partner
        )

    @pl.when(core == 0)
    def _():
        for i in range(K_COUNT):
            doc_copy(i).start()

    k_move = remote(k_hbm, k_core, core_send.at[0], core_recv.at[0], core_partner)
    q_move = remote(q_hbm, q_core, core_send.at[1], core_recv.at[1], core_partner)
    q_load = pltpu.make_async_copy(q_hbm, q, local_sem.at[0])
    k_load = pltpu.make_async_copy(k_hbm, k, local_sem.at[1])
    pair_load = pltpu.make_async_copy(pair_hbm, pair_ref, local_sem.at[2])
    q_load.start()
    k_load.start()
    pair_load.start()

    @pl.when(core == 1)
    def _():
        k_move.start()
        q_move.start()

    q_load.wait()
    k_load.wait()
    pair_load.wait()
    tile_into(s_own, q, k, 0, 2, 256)

    @pl.when(core == 0)
    def _():
        doc_copy(AHEAD).wait_send()
        pl.semaphore_signal(go_sem, inc=1, device_id=core_partner, device_id_type=MESH)
        k_move.start()
        q_move.start()

    @pl.when(core == 1)
    def _():
        pl.semaphore_wait(go_sem, 1)
        for i in range(K_COUNT):
            doc_copy(i).start()

    k_move.wait_recv()
    tile_into(s_right, q, k_core, 0, 2, 256)
    q_move.wait_recv()
    tile_into(s_left, q_core, k, 0, 2, 256)

    top, total = column_partial([s_own, s_left])
    part_out[0:1, :] = top
    part_out[1:2, :] = total
    part_move = remote(part_out, part_in, stat_send.at[0], stat_recv.at[0], far_partner)
    part_move.start()

    top, total = row_partial([s_own, s_right])
    row_top[...] = jnp.broadcast_to(top, row_top.shape)
    row_sum[...] = jnp.broadcast_to(total, row_sum.shape)

    s_far[...] = jnp.zeros_like(s_far)

    @pl.loop(0, K_COUNT)
    def _(i):
        doc_copy(i).wait_recv()
        part = pl.ds(pl.multiple_of(i * K_CHUNK, K_CHUNK), K_CHUNK)
        s_far[...] += logit_scale * lax.dot_general(
            q[:, part], k_far[:, part], (((1,), (1,)), ((), ())), preferred_element_type=jnp.float32
        )

    far_top, far_total = row_partial([s_far])
    near_top = row_top[:, 0:1]
    top = jnp.maximum(near_top, far_top)
    row_lse = top + jnp.log(
        row_sum[:, 0:1] * jnp.exp(near_top - top) + far_total * jnp.exp(far_top - top)
    )
    far_top, far_total = column_partial([s_far])
    part_move.wait_recv()
    near_top = part_in[0:1, :]
    top = jnp.maximum(near_top, far_top)
    far_lse = top + jnp.log(
        part_in[1:2, :] * jnp.exp(near_top - top) + far_total * jnp.exp(far_top - top)
    )
    back_out[0:1, :] = far_lse
    back_move = remote(back_out, back_in, stat_send.at[1], stat_recv.at[1], far_partner)
    back_move.start()
    weights = jnp.exp(s_far[...] - row_lse) + jnp.exp(s_far[...] - far_lse)
    g_far[...] = weights.astype(jnp.bfloat16)
    gt_far[...] = weights.T.astype(jnp.bfloat16)

    @pl.loop(0, P_COUNT)
    def _(i):
        rows = pl.ds(pl.multiple_of(i * P_CHUNK, P_CHUNK), P_CHUNK)
        share_out[rows, :] = dot(gt_far[rows, :], q[...]).astype(jnp.bfloat16)
        share_copy(i).start()

    tail = pl.ds(HEAD, LAST)
    share_out[tail, :] = dot(gt_far[tail, :], q[...]).astype(jnp.bfloat16)
    share_store = pltpu.make_async_copy(share_out.at[tail], share_hbm, out_sem.at[0])
    share_store.start()

    row_out[...] = jnp.broadcast_to(row_lse, row_out.shape)
    row_move = remote(row_out, row_in, stat_send.at[2], stat_recv.at[2], core_partner)
    row_move.start()
    back_move.wait_recv()
    col_out[0:1, :] = back_in[0:1, :]
    col_move = remote(col_out, col_in, stat_send.at[3], stat_recv.at[3], core_partner)
    col_move.start()
    column_lse = back_in[0:1, :]

    row_lse = row_out[:, 0:1]
    pair = jnp.broadcast_to(pair_ref[...].astype(jnp.float32), (128, ROWS)).T[:, 0:1]
    places = lax.broadcasted_iota(jnp.int32, (ROWS, ROWS), 1)
    onehot = (pair.astype(jnp.int32) == places).astype(jnp.float32)
    own = s_own[...]
    weights = jnp.exp(own - row_lse) + jnp.exp(own - column_lse) - 2.0 * onehot
    g_own[...] = weights.astype(jnp.bfloat16)
    gt_own[...] = weights.T.astype(jnp.bfloat16)
    positive = onehot * own
    row_loss = row_lse - positive.sum(axis=1, keepdims=True)
    loss[0:1, :] = jnp.broadcast_to(row_loss, (ROWS, 128)).T[0:1, :]
    loss[1:2, :] = column_lse - positive.sum(axis=0, keepdims=True)

    loss_store = pltpu.make_async_copy(loss, loss_hbm, out_sem.at[3])
    loss_store.start()

    row_move.wait_recv()
    col_move.wait_recv()
    right = s_right[...]
    g_right[...] = (jnp.exp(right - row_lse) + jnp.exp(right - col_in[0:1, :])).astype(jnp.bfloat16)
    left = s_left[...]
    weights = jnp.exp(left - row_in[:, 0:1]) + jnp.exp(left - column_lse)
    gt_left[...] = weights.T.astype(jnp.bfloat16)

    @pl.loop(0, D // WIDE)
    def _(i):
        at = pl.ds(pl.multiple_of(i * WIDE, WIDE), WIDE)
        total = dot(g_own[...], k[:, at]) + dot(g_right[...], k_core[:, at])
        total = total + dot(g_far[...], k_far[:, at])
        dq[:, at] = (logit_scale * total).astype(jnp.bfloat16)
        acc[:, at] = dot(gt_own[...], q[:, at]) + dot(gt_left[...], q_core[:, at])

    dq_store = pltpu.make_async_copy(dq, dq_hbm, out_sem.at[1])
    dq_store.start()
    acc_store = pltpu.make_async_copy(acc.at[tail], acc_hbm, out_sem.at[2])
    acc_store.start()

    def dk_store(i):
        rows = pl.ds(pl.multiple_of(i * P_CHUNK, P_CHUNK), P_CHUNK)
        return pltpu.make_async_copy(dk.at[rows], dk_hbm.at[rows], dk_sem.at[i])

    @pl.loop(0, P_COUNT)
    def _(i):
        share_copy(i).wait_recv()
        rows = pl.ds(pl.multiple_of(i * P_CHUNK, P_CHUNK), P_CHUNK)
        total = acc[rows, :] + share_in[rows, :].astype(jnp.float32)
        dk[rows, :] = (logit_scale * total).astype(jnp.bfloat16)
        dk_store(i).start()

    for i in range(K_COUNT):
        if i != AHEAD:
            doc_copy(i).wait_send()

    @pl.when(core == 1)
    def _():
        doc_copy(AHEAD).wait_send()

    @pl.loop(0, P_COUNT)
    def _(i):
        share_copy(i).wait_send()
        dk_store(i).wait()

    for store in (share_store, dq_store, acc_store, loss_store):
        store.wait()
    for move in (k_move, q_move, part_move, back_move, row_move, col_move):
        move.wait_send()


def settle(dq_in, dk_in, loss_in, dq, dk, row_loss, column_loss, held, loss, load_sem, store_sem, sem):
    parts = [(dq_in, dq, r) for r in range(0, ROWS, SLAB)] + [(dk_in, dk, r) for r in range(0, HEAD, SLAB)]

    def load(i):
        src, _, r = parts[i]
        return pltpu.make_async_copy(src.at[pl.ds(r, SLAB)], held.at[i], load_sem.at[i])

    def store(i):
        _, dst, r = parts[i]
        return pltpu.make_async_copy(held.at[i], dst.at[pl.ds(r, SLAB)], store_sem.at[i])

    loss_load = pltpu.make_async_copy(loss_in, loss, sem)
    loss_load.start()
    for i in range(len(parts)):
        load(i).start()
    loss_load.wait()
    row_loss[...] = loss[0, :]
    column_loss[...] = loss[1, :]
    for i in range(len(parts)):
        load(i).wait()
        store(i).start()
    for i in range(len(parts)):
        store(i).wait()


def finish(acc, share, dk_in, dk, out, sem):
    stores = []
    for r in range(0, LAST, LAST // 4):
        part = pl.ds(r, LAST // 4)
        total = acc[part, :] + share[part, :].astype(jnp.float32)
        out[part, :] = (logit_scale * total).astype(jnp.bfloat16)
        stores.append(pltpu.make_async_copy(out.at[part], dk.at[pl.ds(HEAD + r, LAST // 4)], sem.at[len(stores)]))
        stores[-1].start()
    for store in stores:
        store.wait()


def shards(queries, documents, pair_index):
    vmem = pl.BlockSpec(memory_space=pltpu.VMEM)
    anywhere = pl.BlockSpec(memory_space=pl.ANY)
    f32, bf16 = jnp.float32, jnp.bfloat16
    block = lambda *shape, dtype=bf16: pltpu.VMEM(shape, dtype)
    out = jax.ShapeDtypeStruct
    big = out((ROWS, D), bf16)
    dq, dk_head, share_tail, acc_tail, loss = pl.pallas_call(
        exchange,
        out_shape=(big, out((HEAD, D), bf16), out((LAST, D), bf16), out((LAST, D), f32), out((8, ROWS), f32)),
        in_specs=[anywhere, anywhere, anywhere],
        out_specs=(anywhere, anywhere, anywhere, anywhere, anywhere),
        scratch_shapes=[block(ROWS, D) for _ in range(7)]
        + [block(HEAD, D) for _ in range(2)]
        + [block(ROWS, D, dtype=f32)]
        + [block(ROWS, ROWS, dtype=f32) for _ in range(4)]
        + [block(ROWS, ROWS) for _ in range(6)]
        + [block(ROWS, 128, dtype=f32) for _ in range(4)]
        + [block(8, ROWS, dtype=f32) for _ in range(7)]
        + [block(1, ROWS, dtype=jnp.int32)]
        + [
            pltpu.SemaphoreType.DMA((n,))
            for n in (3, K_COUNT, K_COUNT, 2, 2, 4, 4, P_COUNT, P_COUNT, 4, P_COUNT)
        ]
        + [pltpu.SemaphoreType.REGULAR],
        compiler_params=pltpu.CompilerParams(
            collective_id=0, has_side_effects=True, vmem_limit_bytes=60 << 20
        ),
        cost_estimate=pl.CostEstimate(
            flops=20 * ROWS * ROWS * D, bytes_accessed=16 * ROWS * D, transcendentals=8 * ROWS * ROWS
        ),
    )(queries, documents, pair_index)
    grp_count, dev_count = lax.axis_size("grp"), lax.axis_size("dev")
    route = [(i, i ^ (dev_count // 2)) for i in range(grp_count * dev_count)]
    share = lax.ppermute(share_tail, ("grp", "dev"), route)
    vector = out((ROWS,), f32)
    dq, dk, row_loss, column_loss = pl.pallas_call(
        settle,
        out_shape=(big, big, vector, vector),
        in_specs=[anywhere, anywhere, anywhere],
        out_specs=(anywhere, anywhere, vmem, vmem),
        scratch_shapes=[
            block((ROWS + HEAD) // SLAB, SLAB, D),
            block(8, ROWS, dtype=f32),
            pltpu.SemaphoreType.DMA(((ROWS + HEAD) // SLAB,)),
            pltpu.SemaphoreType.DMA(((ROWS + HEAD) // SLAB,)),
            pltpu.SemaphoreType.DMA,
        ],
        compiler_params=pltpu.CompilerParams(vmem_limit_bytes=60 << 20),
        cost_estimate=pl.CostEstimate(flops=0, bytes_accessed=8 * ROWS * D, transcendentals=0),
    )(dq, dk_head, loss)
    dk = pl.pallas_call(
        finish,
        out_shape=big,
        in_specs=[vmem, vmem, anywhere],
        out_specs=anywhere,
        input_output_aliases={2: 0},
        scratch_shapes=[block(LAST, D), pltpu.SemaphoreType.DMA((4,))],
        compiler_params=pltpu.CompilerParams(vmem_limit_bytes=16 << 20),
        cost_estimate=pl.CostEstimate(flops=2 * LAST * D, bytes_accessed=8 * LAST * D, transcendentals=0),
    )(acc_tail, share, dk)
    return dq, dk, row_loss, column_loss


def solution(mesh):
    rows = P(("grp", "dev"), None)
    flat = P(("grp", "dev"))
    return jax.shard_map(
        shards,
        mesh=mesh,
        in_specs=(rows, rows, rows),
        out_specs=(rows, rows, flat, flat),
        check_vma=False,
    )
```
